32 devices in a mesh: grp: 2 (over y), tile: 8 (over z, x), chan: 2 (over core).
Axes of the slice: x: 2, y: 2, z: 4, core: 2. Of those that a mesh axis runs over, the one named last changes fastest.
Arguments:
- sketch_vectors: bfloat16 [8, 16, 256, 256], P(None, 'tile', 'grp', 'chan'), parts along dimension 2, may hold values from -6 to 6
- base_state: bfloat16 [8, 32, 256], P(None, ('grp', 'tile'), 'chan'), parts along dimension 1, may hold values from -6 to 6
- depth_taps: bfloat16 [3, 9, 256], P(None, None, 'chan'), may hold values from -2 to 2
- mix_weight: bfloat16 [3, 256, 256], P(None, None, 'chan'), may hold values from -0.375 to 0.375
Outputs:
- images: bfloat16 [8, 16, 256, 256], P(None, 'tile', 'grp', 'chan'), parts along dimension 2
- gram: float32 [4, 128, 128], P('grp'), parts along dimension 0
The draws below stay inside these ranges and needn't reach their ends.
There are 2 independent parts, one for each index of `grp`. The reference program is written for one: setup_inputs(seed, part) draws one part's arguments, and reference() takes and returns one part's arrays. A program takes and returns all parts, laid end to end along the dimension named above; an argument that names none is the same for every part. Nothing has to cross between parts.
All inputs are finite; a program needn't handle non-finite values.
Results may differ from the reference program's by a relative error of at most 0.002.
The reference program's roundings to bfloat16 on the way (of `fields` and `conv`) count: a program that leaves them out, or rounds other values in their place, can miss the bound.
Values may be sent and summed in bfloat16 or wider, within the bound.
A program may use at most 64 MiB of HBM per device.

```python
import jax
import jax.numpy as jnp

C = 256
K = 128
LAT = 8
LAYERS = 3
LON = 16


def block_scale(rng, extent, cuts, low, largest):
    factor_of = 1.0
    for dim, shards_of in cuts:
        steps = jax.random.uniform(jax.random.fold_in(jax.random.fold_in(rng, 6), dim), (shards_of,), jnp.float32, low / len(cuts), largest / len(cuts))
        factor_of = factor_of * jnp.repeat(jnp.exp(steps), extent[dim] // shards_of).reshape((-1,) + (1,) * (len(extent) - 1 - dim))
    return factor_of


def normal_values(key, extent, scale, bound, split=(), dtype=jnp.bfloat16):
    level = block_scale(key, extent, split, -0.22, 0.18) if split else 1.0
    values = jax.random.normal(key, extent, jnp.float32) * scale * level
    return jnp.minimum(jnp.maximum(values, -bound), bound).astype(dtype)


def setup_inputs(seed: int = 0, part: int = 0) -> dict:
    seeds = jax.random.split(jax.random.key(seed), 5)
    part_keys = jax.random.split(jax.random.fold_in(seeds[4], part), 5)
    sketch_vectors = normal_values(part_keys[0], (LAT, LON, K, C), 1.0, 6.0, ((1, 8), (3, 2)))
    base_state = normal_values(part_keys[1], (LAT, LON, C), 1.0, 6.0, ((1, 8), (2, 2)))
    depth_taps = normal_values(seeds[2], (LAYERS, 9, C), 9 ** -0.5, 2.0, ((2, 2),))
    mix_weight = normal_values(seeds[3], (LAYERS, C, C), C ** -0.5, 0.375, ((2, 2),))
    return {"sketch_vectors": sketch_vectors, "base_state": base_state, "depth_taps": depth_taps, "mix_weight": mix_weight}


def convolve(fields, tap_rows):
    height = fields.shape[0]
    width = fields.shape[1]
    padded = jnp.pad(fields, ((2, 2), (0, 0), (0, 0), (0, 0)))
    padded = jnp.concatenate([padded[:, -2:], padded, padded[:, :2]], axis=1)
    summed = jnp.zeros(fields.shape, jnp.float32)
    for row_tap in range(3):
        for col_tap in range(3):
            weight_row = tap_rows[3 * row_tap + col_tap].astype(jnp.float32)
            window = padded[2 * row_tap:2 * row_tap + height, 2 * col_tap:2 * col_tap + width]
            summed = summed + weight_row * window.astype(jnp.float32)
    return summed.astype(jnp.bfloat16)


def reference(sketch_vectors, base_state, depth_taps, mix_weight):
    fields = jnp.concatenate([base_state[:, :, None, :], sketch_vectors], axis=2)
    for layer in range(LAYERS):
        conv = convolve(fields, depth_taps[layer])
        mixed = jnp.dot(conv, mix_weight[layer], preferred_element_type=jnp.float32)
        slope = jnp.tanh(mixed[:, :, 0:1, :])
        base_next = fields[:, :, 0:1, :].astype(jnp.float32) + slope
        vec_next = fields[:, :, 1:, :].astype(jnp.float32) + (1.0 - slope * slope) * mixed[:, :, 1:, :]
        fields = jnp.concatenate([base_next, vec_next], axis=2).astype(jnp.bfloat16)
    images = fields[:, :, 1:, :]
    flat_images = images.reshape(-1, K, C).astype(jnp.float32)
    flat_sketch = sketch_vectors.reshape(-1, K, C).astype(jnp.float32)
    scale = 1.0 / (LAT * LON * C)
    first = jnp.einsum('pkc,pjc->kj', flat_images, flat_images) * scale
    second = jnp.einsum('pkc,pjc->kj', flat_sketch, flat_images) * scale
    return images, jnp.stack([first, second])
```

```python
import functools

import jax
import jax.numpy as jnp
from jax import lax
from jax.experimental import pallas as pl
from jax.experimental.pallas import tpu as pltpu
from jax.sharding import PartitionSpec as P

LAYERS = 3
MESH = pl.DeviceIdType.MESH
BF16 = jnp.bfloat16
F32 = jnp.float32


def extended_2(block, sides, width):
    for axis, dim in sides:
        count = lax.axis_size(axis)
        forward = [(i, i + 1) for i in range(count - 1)]
        forward.append((count - 1, 0))
        backward = [(target, source) for source, target in forward]
        low = lax.ppermute(
            lax.slice_in_dim(block, block.shape[dim] - width, None, axis=dim), axis, forward
        )
        high = lax.ppermute(lax.slice_in_dim(block, 0, width, axis=dim), axis, backward)
        block = jnp.concatenate([low, block, high], axis=dim)
    return block


def convolve(extended, tap_rows, width):
    height = extended.shape[0]
    padded = jnp.pad(extended, ((2, 2), (0, 0), (0, 0), (0, 0)))
    summed = jnp.zeros((height, width) + extended.shape[2:], jnp.float32)
    for row_tap in range(3):
        for col_tap in range(3):
            weight_row = tap_rows[3 * row_tap + col_tap].astype(jnp.float32)
            window = padded[2 * row_tap : 2 * row_tap + height, 2 * col_tap : 2 * col_tap + width]
            summed = summed + weight_row * window.astype(jnp.float32)
    return summed.astype(jnp.bfloat16)


def advance(fields, mixed):
    slope = jnp.tanh(mixed[:, :, 0:1, :])
    base_next = fields[:, :, 0:1, :].astype(jnp.float32) + slope
    vec_next = fields[:, :, 1:, :].astype(jnp.float32) + (1.0 - slope * slope) * mixed[:, :, 1:, :]
    return jnp.concatenate([base_next, vec_next], axis=2).astype(jnp.bfloat16)


def per_device(sketch_vectors, base_state, depth_taps, mix_weight):
    width = sketch_vectors.shape[1]
    fields = jnp.concatenate([base_state[:, :, None, :], sketch_vectors], axis=2)
    for layer in range(LAYERS):
        extended = extended_2(fields, (("tile", 1),), 2)
        conv = convolve(extended, depth_taps[layer], width)
        layer_mix = mix_weight[layer]
        mixed = jnp.dot(
            lax.all_gather(conv, "chan", axis=3, tiled=True),
            layer_mix,
            preferred_element_type=jnp.float32,
        )
        fields = advance(fields, mixed)
    images = fields[:, :, 1:, :]
    num_vectors = images.shape[2]
    flat_images = images.reshape(-1, num_vectors, images.shape[3])
    flat_sketch = sketch_vectors.reshape(-1, num_vectors, images.shape[3])
    first = jnp.einsum("pkc,pjc->kj", flat_images, flat_images, preferred_element_type=jnp.float32)
    second = jnp.einsum("pkc,pjc->kj", flat_sketch, flat_images, preferred_element_type=jnp.float32)
    total_cells = (
        images.shape[0] * width * lax.axis_size("tile") * images.shape[3] * lax.axis_size("chan")
    )
    summed = lax.psum(jnp.stack([first, second]), ("tile", "chan"))
    return (images, summed / total_cells)


def transposed_kernel(
    tiles, chans, scale, sk_hbm, base_ref, taps_ref, mix_hbm, img_hbm, gram_ref,
    fields, sketch, img, weights, taps, base_rows, base_all, conv, gain, acc, part, total,
    local_sem, own_sem, base_send, base_recv, pair_send, pair_recv,
    in_send, in_recv, out_send, out_recv, red_send, red_recv, all_send, all_recv,
):
    group, tile, chan = lax.axis_index("grp"), lax.axis_index("tile"), lax.axis_index("chan")
    count = tiles * chans
    me = tile * chans + chan
    rows, _, _, num_vectors, width = sk_hbm.shape
    per_tile = num_vectors // tiles
    channels = chans * width
    share = 2 * num_vectors // count

    def device(index):
        return lax.div(index, chans), lax.rem(index, chans)

    def target(step):
        return device(lax.rem(me + step, count))

    def source(step):
        return device(lax.rem(me - step + count, count))

    def lanes(c):
        return pl.ds(pl.multiple_of(c * width, width), width)

    def vectors(t):
        return pl.ds(pl.multiple_of(t * per_tile, per_tile), per_tile)

    def share_of(index):
        return pl.ds(pl.multiple_of(index * share, share), share)

    def remote(src, dst, send, recv, to):
        return pltpu.make_async_remote_copy(
            src_ref=src, dst_ref=dst, send_sem=send, recv_sem=recv,
            device_id=(group, to[0], to[1]), device_id_type=MESH,
        )

    def each_step(body):
        def wrapped(step, carry):
            body(step)
            return carry

        lax.fori_loop(1, count, wrapped, 0)

    def copy_in(parity, step, to, of):
        return remote(
            sk_hbm.at[:, parity, to[1], vectors(to[0]), :],
            fields.at[parity, of[0], :, :, lanes(of[1])],
            in_send.at[parity, step], in_recv.at[parity, step], to,
        )

    def copy_out(parity, step, to, of):
        return remote(
            fields.at[parity, to[0], :, :, lanes(to[1])],
            img.at[parity, of[1], :, vectors(of[0]), :],
            out_send.at[parity, step], out_recv.at[parity, step], to,
        )

    def copy_base(step, to, of):
        return remote(
            base_all.at[tile, chan], base_all.at[of[0], of[1]],
            base_send.at[step], base_recv.at[step], to,
        )

    def copy_part(step, to):
        return remote(
            acc.at[share_of(to[0] * chans + to[1])], part.at[step],
            red_send.at[step], red_recv.at[step], to,
        )

    def copy_total(step, to, of):
        return remote(
            total.at[share_of(me)], total.at[share_of(of[0] * chans + of[1])],
            all_send.at[step], all_recv.at[step], to,
        )

    mine = (tile, chan)
    barrier = pltpu.get_barrier_semaphore()

    def greet(step):
        to = target(step)
        pl.semaphore_signal(barrier, inc=1, device_id=(group, to[0], to[1]), device_id_type=MESH)

    each_step(greet)

    weights_here = pltpu.make_async_copy(mix_hbm, weights.at[:, :, lanes(chan)], local_sem.at[0])
    sketch_here = pltpu.make_async_copy(sk_hbm, sketch, local_sem.at[1])
    own_in = [
        pltpu.make_async_copy(
            sk_hbm.at[:, parity, chan, vectors(tile), :],
            fields.at[parity, tile, :, :, lanes(chan)],
            own_sem.at[0, parity],
        )
        for parity in range(2)
    ]
    weights_here.start()
    own_in[0].start()
    own_in[1].start()
    sketch_here.start()

    taps[:, :, lanes(chan)] = jnp.zeros((LAYERS, 16, width), F32)
    for layer in range(LAYERS):
        taps[layer, 0:9, lanes(chan)] = taps_ref[layer].astype(F32)
    lat = base_ref.shape[0]
    for row in range(lat):
        pair = base_ref[row].astype(F32)
        for parity in range(2):
            base_rows[parity * lat + row : parity * lat + row + 1, :] = pair[parity : parity + 1]
    base_all[tile, chan] = base_rows[...].astype(BF16)

    pl.semaphore_wait(barrier, count - 1)

    each_step(lambda step: copy_base(step, target(step), mine).start())
    other = (tile, lax.rem(chan + 1, chans))

    def copy_taps(of):
        return remote(
            taps.at[:, :, lanes(chan)], taps.at[:, :, lanes(of[1])],
            pair_send.at[0], pair_recv.at[0], other,
        )

    def copy_weights(of):
        return remote(
            mix_hbm, weights.at[:, :, lanes(of[1])], pair_send.at[1], pair_recv.at[1], other
        )

    copy_taps(mine).start()
    copy_weights(mine).start()
    for parity in range(2):
        each_step(lambda step: copy_in(parity, step, target(step), mine).start())

    copy_taps(other).wait_recv()
    copy_weights(other).wait_recv()
    weights_here.wait()
    each_step(lambda step: copy_base(step, target(step), source(step)).wait_recv())
    base = []
    for t in range(tiles):
        halves = []
        for c in range(chans):
            both = base_all[t, c].astype(F32)
            halves.append(jnp.where(chan == 0, both[:lat], both[lat:]))
        base.append(jnp.concatenate(halves, axis=1))
    edge = jnp.zeros((2, channels), F32)
    for layer in range(LAYERS):
        summed = []
        for t in range(tiles):
            by_row = []
            for a in range(3):
                row_sum = None
                for b in range(3):
                    tap = taps[layer, 3 * a + b : 3 * a + b + 1, :]
                    term = tap * base[(t + b - 1) % tiles]
                    row_sum = term if row_sum is None else row_sum + term
                by_row.append(row_sum)
            summed.append(
                jnp.concatenate([edge, by_row[0][: lat - 2]], axis=0)
                + by_row[1]
                + jnp.concatenate([by_row[2][2:], edge], axis=0)
            )
        mixed = jnp.dot(
            jnp.concatenate(summed, axis=0).astype(BF16), weights[layer],
            preferred_element_type=F32,
        )
        slope = jnp.tanh(mixed)
        gain[layer] = 1.0 - slope * slope
        base = [
            (base[t] + slope[t * lat : (t + 1) * lat]).astype(BF16).astype(F32)
            for t in range(tiles)
        ]

    def run_layers(parity):
        for layer in range(LAYERS):

            def convolve_tile(t, carry):
                near = (lax.rem(t + tiles - 1, tiles), t, lax.rem(t + 1, tiles))
                for c in range(chans):
                    part_lanes = slice(c * width, (c + 1) * width)
                    cols = [fields[parity, n, :, :, part_lanes].astype(F32) for n in near]
                    for row in range(rows):
                        summed = None
                        for a in range(3):
                            if not 0 <= row + a - 1 < rows:
                                continue
                            for b in range(3):
                                tap = taps[layer, 3 * a + b : 3 * a + b + 1, part_lanes]
                                term = tap * cols[b][row + a - 1]
                                summed = term if summed is None else summed + term
                        conv[t, row * per_tile : (row + 1) * per_tile, part_lanes] = (
                            summed.astype(BF16)
                        )
                return carry

            lax.fori_loop(0, tiles, convolve_tile, 0)
            step = 4 if tiles % 4 == 0 else 1

            def mix_tiles(block, carry):
                first = block * step
                cells = conv[pl.ds(first, step)].reshape(step * rows * per_tile, channels)
                mixed = jnp.dot(cells, weights[layer], preferred_element_type=F32)
                for n in range(step):
                    for row in range(rows):
                        at = (n * rows + row) * per_tile
                        factor = gain[layer, pl.ds((first + n) * lat + 2 * row + parity, 1), :]
                        fields[parity, first + n, row] = (
                            fields[parity, first + n, row].astype(F32)
                            + factor * mixed[at : at + per_tile]
                        ).astype(BF16)
                return carry

            lax.fori_loop(0, tiles // step, mix_tiles, 0)

    own_out = [
        pltpu.make_async_copy(
            fields.at[parity, tile, :, :, lanes(chan)],
            img.at[parity, chan, :, vectors(tile), :],
            own_sem.at[1, parity],
        )
        for parity in range(2)
    ]
    for parity in range(2):
        own_in[parity].wait()
        each_step(lambda step: copy_in(parity, step, target(step), source(step)).wait_recv())
        run_layers(parity)
        own_out[parity].start()
        each_step(lambda step: copy_out(parity, step, target(step), mine).start())

    sketch_here.wait()
    images_out = []
    grams = jnp.zeros((2 * num_vectors, num_vectors), F32)
    for parity in range(2):
        own_out[parity].wait()
        each_step(lambda step: copy_out(parity, step, target(step), source(step)).wait_recv())
        for lon in range(2):
            out = pltpu.make_async_copy(
                img.at[parity, lon], img_hbm.at[:, parity, lon], local_sem.at[2 + 2 * parity + lon]
            )
            out.start()
            images_out.append(out)
        for row in range(rows):
            here = jnp.concatenate([img[parity, 0, row], img[parity, 1, row]], axis=1)
            start = jnp.concatenate([sketch[row, parity, 0], sketch[row, parity, 1]], axis=1)
            grams = grams + lax.dot_general(
                jnp.concatenate([here, start], axis=0), here, (((1,), (1,)), ((), ())),
                preferred_element_type=F32,
            )
    acc[...] = grams
    each_step(lambda step: copy_part(step, target(step)).start())
    each_step(lambda step: copy_part(step, target(step)).wait_recv())
    summed = acc[share_of(me), :]
    for step in range(1, count):
        summed = summed + part[step]
    total[share_of(me), :] = summed * scale
    each_step(lambda step: copy_total(step, target(step), mine).start())

    copy_taps(mine).wait_send()
    copy_weights(mine).wait_send()
    each_step(lambda step: copy_base(step, target(step), mine).wait_send())
    for parity in range(2):
        each_step(lambda step: copy_in(parity, step, target(step), mine).wait_send())
        each_step(lambda step: copy_out(parity, step, target(step), mine).wait_send())
    each_step(lambda step: copy_part(step, target(step)).wait_send())
    for out in images_out:
        out.wait()
    each_step(lambda step: copy_total(step, target(step), source(step)).wait_recv())
    gram_ref[0] = total[:num_vectors]
    gram_ref[1] = total[num_vectors:]
    each_step(lambda step: copy_total(step, target(step), mine).wait_send())


def per_device_transposed(sketch_vectors, base_state, depth_taps, mix_weight):
    tiles, chans = lax.axis_size("tile"), lax.axis_size("chan")
    count = tiles * chans
    lat, lon, num_vectors, width = sketch_vectors.shape
    rows = lat // 2
    per_tile = num_vectors // tiles
    channels = chans * width
    scale = 1.0 / (lat * lon * tiles * channels)
    split = sketch_vectors.reshape(rows, 2, lon, num_vectors, width)
    images, gram = pl.pallas_call(
        functools.partial(transposed_kernel, tiles, chans, scale),
        out_shape=(
            jax.ShapeDtypeStruct(split.shape, BF16),
            jax.ShapeDtypeStruct((2, num_vectors, num_vectors), F32),
        ),
        in_specs=[
            pl.BlockSpec(memory_space=pl.ANY),
            pl.BlockSpec(memory_space=pltpu.VMEM),
            pl.BlockSpec(memory_space=pltpu.VMEM),
            pl.BlockSpec(memory_space=pl.ANY),
        ],
        out_specs=(pl.BlockSpec(memory_space=pl.ANY), pl.BlockSpec(memory_space=pltpu.VMEM)),
        scratch_shapes=[
            pltpu.VMEM((2, tiles, rows, per_tile, channels), BF16),
            pltpu.VMEM(split.shape, BF16),
            pltpu.VMEM((2, lon, rows, num_vectors, width), BF16),
            pltpu.VMEM((LAYERS, channels, channels), BF16),
            pltpu.VMEM((LAYERS, 16, channels), F32),
            pltpu.VMEM((2 * lat, width), F32),
            pltpu.VMEM((tiles, chans, 2 * lat, width), BF16),
            pltpu.VMEM((tiles, rows * per_tile, channels), BF16),
            pltpu.VMEM((LAYERS, tiles * lat, channels), F32),
            pltpu.VMEM((2 * num_vectors, num_vectors), F32),
            pltpu.VMEM((count, 2 * num_vectors // count, num_vectors), F32),
            pltpu.VMEM((2 * num_vectors, num_vectors), F32),
            pltpu.SemaphoreType.DMA((6,)),
            pltpu.SemaphoreType.DMA((2, 2)),
            pltpu.SemaphoreType.DMA((count,)),
            pltpu.SemaphoreType.DMA((count,)),
            pltpu.SemaphoreType.DMA((2,)),
            pltpu.SemaphoreType.DMA((2,)),
            pltpu.SemaphoreType.DMA((2, count)),
            pltpu.SemaphoreType.DMA((2, count)),
            pltpu.SemaphoreType.DMA((2, count)),
            pltpu.SemaphoreType.DMA((2, count)),
            pltpu.SemaphoreType.DMA((count,)),
            pltpu.SemaphoreType.DMA((count,)),
            pltpu.SemaphoreType.DMA((count,)),
            pltpu.SemaphoreType.DMA((count,)),
        ],
        compiler_params=pltpu.CompilerParams(
            collective_id=0, has_side_effects=True, vmem_limit_bytes=32 * 1024 * 1024
        ),
    )(split, base_state, depth_taps, mix_weight)
    return images.reshape(sketch_vectors.shape), gram


def fits_transposed(shape, mesh_shape):
    lat, lon, num_vectors, width = shape
    tiles, chans = mesh_shape["tile"], mesh_shape["chan"]
    return (
        lat == 8 and lon == 2 and chans == 2 and width % 128 == 0
        and num_vectors == width == 128 and tiles > 1
        and num_vectors % (16 * tiles) == 0 and (2 * num_vectors) % (8 * tiles * chans) == 0
    )


def local_step(mesh_shape, *args):
    if fits_transposed(args[0].shape, mesh_shape):
        return per_device_transposed(*args)
    return per_device(*args)


def solution(mesh):
    in_specs = (
        P(None, "tile", "grp", "chan"),
        P(None, ("grp", "tile"), "chan"),
        P(None, None, "chan"),
        P(None, None, "chan"),
    )
    out_specs = (P(None, "tile", "grp", "chan"), P("grp", None, None))
    return jax.shard_map(
        functools.partial(local_step, dict(mesh.shape)), mesh=mesh, in_specs=in_specs, out_specs=out_specs, check_vma=False
    )
```

```python
import functools

import jax
import jax.numpy as jnp
from jax import lax
from jax.experimental import pallas as pl
from jax.experimental.pallas import tpu as pltpu
from jax.sharding import PartitionSpec as P

LAYERS = 3
MESH = pl.DeviceIdType.MESH
BF16 = jnp.bfloat16
F32 = jnp.float32


def extended_2(block, sides, width):
    for axis, dim in sides:
        count = lax.axis_size(axis)
        forward = [(i, i + 1) for i in range(count - 1)]
        forward.append((count - 1, 0))
        backward = [(target, source) for source, target in forward]
        low = lax.ppermute(
            lax.slice_in_dim(block, block.shape[dim] - width, None, axis=dim), axis, forward
        )
        high = lax.ppermute(lax.slice_in_dim(block, 0, width, axis=dim), axis, backward)
        block = jnp.concatenate([low, block, high], axis=dim)
    return block


def convolve(extended, tap_rows, width):
    height = extended.shape[0]
    padded = jnp.pad(extended, ((2, 2), (0, 0), (0, 0), (0, 0)))
    summed = jnp.zeros((height, width) + extended.shape[2:], jnp.float32)
    for row_tap in range(3):
        for col_tap in range(3):
            weight_row = tap_rows[3 * row_tap + col_tap].astype(jnp.float32)
            window = padded[2 * row_tap : 2 * row_tap + height, 2 * col_tap : 2 * col_tap + width]
            summed = summed + weight_row * window.astype(jnp.float32)
    return summed.astype(jnp.bfloat16)


def advance(fields, mixed):
    slope = jnp.tanh(mixed[:, :, 0:1, :])
    base_next = fields[:, :, 0:1, :].astype(jnp.float32) + slope
    vec_next = fields[:, :, 1:, :].astype(jnp.float32) + (1.0 - slope * slope) * mixed[:, :, 1:, :]
    return jnp.concatenate([base_next, vec_next], axis=2).astype(jnp.bfloat16)


def per_device(sketch_vectors, base_state, depth_taps, mix_weight):
    width = sketch_vectors.shape[1]
    fields = jnp.concatenate([base_state[:, :, None, :], sketch_vectors], axis=2)
    for layer in range(LAYERS):
        extended = extended_2(fields, (("tile", 1),), 2)
        conv = convolve(extended, depth_taps[layer], width)
        layer_mix = mix_weight[layer]
        mixed = jnp.dot(
            lax.all_gather(conv, "chan", axis=3, tiled=True),
            layer_mix,
            preferred_element_type=jnp.float32,
        )
        fields = advance(fields, mixed)
    images = fields[:, :, 1:, :]
    num_vectors = images.shape[2]
    flat_images = images.reshape(-1, num_vectors, images.shape[3])
    flat_sketch = sketch_vectors.reshape(-1, num_vectors, images.shape[3])
    first = jnp.einsum("pkc,pjc->kj", flat_images, flat_images, preferred_element_type=jnp.float32)
    second = jnp.einsum("pkc,pjc->kj", flat_sketch, flat_images, preferred_element_type=jnp.float32)
    total_cells = (
        images.shape[0] * width * lax.axis_size("tile") * images.shape[3] * lax.axis_size("chan")
    )
    summed = lax.psum(jnp.stack([first, second]), ("tile", "chan"))
    return (images, summed / total_cells)


def transposed_kernel(
    tiles, chans, scale, sk_hbm, base_ref, taps_ref, mix_hbm, img_hbm, gram_ref,
    fields, sketch, img, weights, taps, base_rows, base_all, conv, gain, acc, paired, part, total,
    local_sem, own_sem, base_send, base_recv, pair_send, pair_recv,
    in_send, in_recv, out_send, out_recv, red_send, red_recv, all_send, all_recv,
):
    group, tile, chan = lax.axis_index("grp"), lax.axis_index("tile"), lax.axis_index("chan")
    count = tiles * chans
    me = tile * chans + chan
    rows, _, _, num_vectors, width = sk_hbm.shape
    per_tile = num_vectors // tiles
    channels = chans * width
    share = num_vectors // tiles

    def device(index):
        return lax.div(index, chans), lax.rem(index, chans)

    def target(step):
        return device(lax.rem(me + step, count))

    def source(step):
        return device(lax.rem(me - step + count, count))

    def lanes(c):
        return pl.ds(pl.multiple_of(c * width, width), width)

    def vectors(t):
        return pl.ds(pl.multiple_of(t * per_tile, per_tile), per_tile)

    def share_of(index):
        return pl.ds(pl.multiple_of(index * share, share), share)

    def remote(src, dst, send, recv, to):
        return pltpu.make_async_remote_copy(
            src_ref=src, dst_ref=dst, send_sem=send, recv_sem=recv,
            device_id=(group, to[0], to[1]), device_id_type=MESH,
        )

    def each_step(body):
        def wrapped(step, carry):
            body(step)
            return carry

        lax.fori_loop(1, count, wrapped, 0)

    def each_tile(body):
        def wrapped(step, carry):
            body(step)
            return carry

        lax.fori_loop(1, tiles, wrapped, 0)

    def next_tile(step):
        return lax.rem(tile + step, tiles), chan

    def copy_in(parity, step, to, of):
        return remote(
            sk_hbm.at[:, parity, to[1], vectors(to[0]), :],
            fields.at[parity, of[0], :, :, lanes(of[1])],
            in_send.at[parity, step], in_recv.at[parity, step], to,
        )

    def copy_out(parity, step, to, of):
        return remote(
            fields.at[parity, to[0], :, :, lanes(to[1])],
            img.at[parity, of[1], :, vectors(of[0]), :],
            out_send.at[parity, step], out_recv.at[parity, step], to,
        )

    def copy_base(step, to, of):
        return remote(
            base_all.at[tile, chan], base_all.at[of[0], of[1]],
            base_send.at[step], base_recv.at[step], to,
        )

    def copy_part(step, to):
        return remote(
            paired.at[0, share_of(to[0])], part.at[step], red_send.at[step], red_recv.at[step], to
        )

    def copy_total(step, to, of):
        return remote(
            total.at[chan, share_of(tile)], total.at[of[1], share_of(of[0])],
            all_send.at[step], all_recv.at[step], to,
        )

    mine = (tile, chan)
    barrier = pltpu.get_barrier_semaphore()

    def greet(step):
        to = target(step)
        pl.semaphore_signal(barrier, inc=1, device_id=(group, to[0], to[1]), device_id_type=MESH)

    each_step(greet)

    weights_here = pltpu.make_async_copy(mix_hbm, weights.at[:, :, lanes(chan)], local_sem.at[0])
    sketch_here = pltpu.make_async_copy(sk_hbm, sketch, local_sem.at[1])
    own_in = [
        pltpu.make_async_copy(
            sk_hbm.at[:, parity, chan, vectors(tile), :],
            fields.at[parity, tile, :, :, lanes(chan)],
            own_sem.at[0, parity],
        )
        for parity in range(2)
    ]
    weights_here.start()
    own_in[0].start()
    own_in[1].start()
    sketch_here.start()

    taps[:, :, lanes(chan)] = jnp.zeros((LAYERS, 16, width), F32)
    for layer in range(LAYERS):
        taps[layer, 0:9, lanes(chan)] = taps_ref[layer].astype(F32)
    lat = base_ref.shape[0]
    for row in range(lat):
        pair = base_ref[row].astype(F32)
        for parity in range(2):
            base_rows[parity * lat + row : parity * lat + row + 1, :] = pair[parity : parity + 1]
    base_all[tile, chan] = base_rows[...].astype(BF16)

    pl.semaphore_wait(barrier, count - 1)

    each_step(lambda step: copy_base(step, target(step), mine).start())
    other = (tile, lax.rem(chan + 1, chans))

    def copy_taps(of):
        return remote(
            taps.at[:, :, lanes(chan)], taps.at[:, :, lanes(of[1])],
            pair_send.at[0], pair_recv.at[0], other,
        )

    def copy_weights(of):
        return remote(
            mix_hbm, weights.at[:, :, lanes(of[1])], pair_send.at[1], pair_recv.at[1], other
        )

    copy_taps(mine).start()
    copy_weights(mine).start()
    for parity in range(2):
        each_step(lambda step: copy_in(parity, step, target(step), mine).start())

    copy_taps(other).wait_recv()
    copy_weights(other).wait_recv()
    weights_here.wait()
    each_step(lambda step: copy_base(step, target(step), source(step)).wait_recv())
    base = []
    for t in range(tiles):
        halves = []
        for c in range(chans):
            both = base_all[t, c].astype(F32)
            halves.append(jnp.where(chan == 0, both[:lat], both[lat:]))
        base.append(jnp.concatenate(halves, axis=1))
    edge = jnp.zeros((2, channels), F32)
    for layer in range(LAYERS):
        summed = []
        for t in range(tiles):
            by_row = []
            for a in range(3):
                row_sum = None
                for b in range(3):
                    tap = taps[layer, 3 * a + b : 3 * a + b + 1, :]
                    term = tap * base[(t + b - 1) % tiles]
                    row_sum = term if row_sum is None else row_sum + term
                by_row.append(row_sum)
            summed.append(
                jnp.concatenate([edge, by_row[0][: lat - 2]], axis=0)
                + by_row[1]
                + jnp.concatenate([by_row[2][2:], edge], axis=0)
            )
        mixed = jnp.dot(
            jnp.concatenate(summed, axis=0).astype(BF16), weights[layer],
            preferred_element_type=F32,
        )
        slope = jnp.tanh(mixed)
        gain[layer] = 1.0 - slope * slope
        base = [
            (base[t] + slope[t * lat : (t + 1) * lat]).astype(BF16).astype(F32)
            for t in range(tiles)
        ]

    def run_layers(parity):
        for layer in range(LAYERS):

            def convolve_tile(t, carry):
                near = (lax.rem(t + tiles - 1, tiles), t, lax.rem(t + 1, tiles))
                for c in range(chans):
                    part_lanes = slice(c * width, (c + 1) * width)
                    cols = [fields[parity, n, :, :, part_lanes].astype(F32) for n in near]
                    for row in range(rows):
                        summed = None
                        for a in range(3):
                            if not 0 <= row + a - 1 < rows:
                                continue
                            for b in range(3):
                                tap = taps[layer, 3 * a + b : 3 * a + b + 1, part_lanes]
                                term = tap * cols[b][row + a - 1]
                                summed = term if summed is None else summed + term
                        conv[t, row * per_tile : (row + 1) * per_tile, part_lanes] = (
                            summed.astype(BF16)
                        )
                return carry

            lax.fori_loop(0, tiles, convolve_tile, 0)
            step = 4 if tiles % 4 == 0 else 1

            def mix_tiles(block, carry):
                first = block * step
                cells = conv[pl.ds(first, step)].reshape(step * rows * per_tile, channels)
                mixed = jnp.dot(cells, weights[layer], preferred_element_type=F32)
                for n in range(step):
                    for row in range(rows):
                        at = (n * rows + row) * per_tile
                        factor = gain[layer, pl.ds((first + n) * lat + 2 * row + parity, 1), :]
                        fields[parity, first + n, row] = (
                            fields[parity, first + n, row].astype(F32)
                            + factor * mixed[at : at + per_tile]
                        ).astype(BF16)
                return carry

            lax.fori_loop(0, tiles // step, mix_tiles, 0)

    own_out = [
        pltpu.make_async_copy(
            fields.at[parity, tile, :, :, lanes(chan)],
            img.at[parity, chan, :, vectors(tile), :],
            own_sem.at[1, parity],
        )
        for parity in range(2)
    ]
    for parity in range(2):
        own_in[parity].wait()
        each_step(lambda step: copy_in(parity, step, target(step), source(step)).wait_recv())
        run_layers(parity)
        own_out[parity].start()
        each_step(lambda step: copy_out(parity, step, target(step), mine).start())

    sketch_here.wait()
    images_out = []
    grams = jnp.zeros((2 * num_vectors, num_vectors), F32)
    for parity in range(2):
        own_out[parity].wait()
        each_step(lambda step: copy_out(parity, step, target(step), source(step)).wait_recv())
        for lon in range(2):
            out = pltpu.make_async_copy(
                img.at[parity, lon], img_hbm.at[:, parity, lon], local_sem.at[2 + 2 * parity + lon]
            )
            out.start()
            images_out.append(out)
        for row in range(rows):
            here = jnp.concatenate([img[parity, 0, row], img[parity, 1, row]], axis=1)
            start = jnp.concatenate([sketch[row, parity, 0], sketch[row, parity, 1]], axis=1)
            grams = grams + lax.dot_general(
                jnp.concatenate([here, start], axis=0), here, (((1,), (1,)), ((), ())),
                preferred_element_type=F32,
            )
    acc[0] = grams[:num_vectors]
    acc[1] = grams[num_vectors:]
    swap = remote(
        acc.at[lax.rem(chan + 1, chans)], paired.at[1], pair_send.at[2], pair_recv.at[2], other
    )
    swap.start()
    swap.wait_recv()
    paired[0] = acc[chan] + paired[1]
    each_tile(lambda step: copy_part(step, next_tile(step)).start())
    each_tile(lambda step: copy_part(step, next_tile(step)).wait_recv())
    summed = paired[0, share_of(tile), :]
    for step in range(1, tiles):
        summed = summed + part[step]
    total[chan, share_of(tile), :] = summed * scale
    each_step(lambda step: copy_total(step, target(step), mine).start())

    copy_taps(mine).wait_send()
    copy_weights(mine).wait_send()
    each_step(lambda step: copy_base(step, target(step), mine).wait_send())
    for parity in range(2):
        each_step(lambda step: copy_in(parity, step, target(step), mine).wait_send())
        each_step(lambda step: copy_out(parity, step, target(step), mine).wait_send())
    swap.wait_send()
    each_tile(lambda step: copy_part(step, next_tile(step)).wait_send())
    for out in images_out:
        out.wait()
    each_step(lambda step: copy_total(step, target(step), source(step)).wait_recv())
    gram_ref[...] = total[...]
    each_step(lambda step: copy_total(step, target(step), mine).wait_send())


def per_device_transposed(sketch_vectors, base_state, depth_taps, mix_weight):
    tiles, chans = lax.axis_size("tile"), lax.axis_size("chan")
    count = tiles * chans
    lat, lon, num_vectors, width = sketch_vectors.shape
    rows = lat // 2
    per_tile = num_vectors // tiles
    channels = chans * width
    scale = 1.0 / (lat * lon * tiles * channels)
    split = sketch_vectors.reshape(rows, 2, lon, num_vectors, width)
    images, gram = pl.pallas_call(
        functools.partial(transposed_kernel, tiles, chans, scale),
        out_shape=(
            jax.ShapeDtypeStruct(split.shape, BF16),
            jax.ShapeDtypeStruct((2, num_vectors, num_vectors), F32),
        ),
        in_specs=[
            pl.BlockSpec(memory_space=pl.ANY),
            pl.BlockSpec(memory_space=pltpu.VMEM),
            pl.BlockSpec(memory_space=pltpu.VMEM),
            pl.BlockSpec(memory_space=pl.ANY),
        ],
        out_specs=(pl.BlockSpec(memory_space=pl.ANY), pl.BlockSpec(memory_space=pltpu.VMEM)),
        scratch_shapes=[
            pltpu.VMEM((2, tiles, rows, per_tile, channels), BF16),
            pltpu.VMEM(split.shape, BF16),
            pltpu.VMEM((2, lon, rows, num_vectors, width), BF16),
            pltpu.VMEM((LAYERS, channels, channels), BF16),
            pltpu.VMEM((LAYERS, 16, channels), F32),
            pltpu.VMEM((2 * lat, width), F32),
            pltpu.VMEM((tiles, chans, 2 * lat, width), BF16),
            pltpu.VMEM((tiles, rows * per_tile, channels), BF16),
            pltpu.VMEM((LAYERS, tiles * lat, channels), F32),
            pltpu.VMEM((2, num_vectors, num_vectors), F32),
            pltpu.VMEM((2, num_vectors, num_vectors), F32),
            pltpu.VMEM((tiles, num_vectors // tiles, num_vectors), F32),
            pltpu.VMEM((2, num_vectors, num_vectors), F32),
            pltpu.SemaphoreType.DMA((6,)),
            pltpu.SemaphoreType.DMA((2, 2)),
            pltpu.SemaphoreType.DMA((count,)),
            pltpu.SemaphoreType.DMA((count,)),
            pltpu.SemaphoreType.DMA((3,)),
            pltpu.SemaphoreType.DMA((3,)),
            pltpu.SemaphoreType.DMA((2, count)),
            pltpu.SemaphoreType.DMA((2, count)),
            pltpu.SemaphoreType.DMA((2, count)),
            pltpu.SemaphoreType.DMA((2, count)),
            pltpu.SemaphoreType.DMA((count,)),
            pltpu.SemaphoreType.DMA((count,)),
            pltpu.SemaphoreType.DMA((count,)),
            pltpu.SemaphoreType.DMA((count,)),
        ],
        compiler_params=pltpu.CompilerParams(
            collective_id=0, has_side_effects=True, vmem_limit_bytes=32 * 1024 * 1024
        ),
    )(split, base_state, depth_taps, mix_weight)
    return images.reshape(sketch_vectors.shape), gram


def fits_transposed(shape, mesh_shape):
    lat, lon, num_vectors, width = shape
    tiles, chans = mesh_shape["tile"], mesh_shape["chan"]
    return (
        lat == 8 and lon == 2 and chans == 2 and width % 128 == 0
        and num_vectors == width == 128 and tiles > 1
        and num_vectors % (16 * tiles) == 0 and lon == chans
    )


def local_step(mesh_shape, *args):
    if fits_transposed(args[0].shape, mesh_shape):
        return per_device_transposed(*args)
    return per_device(*args)


def solution(mesh):
    in_specs = (
        P(None, "tile", "grp", "chan"),
        P(None, ("grp", "tile"), "chan"),
        P(None, None, "chan"),
        P(None, None, "chan"),
    )
    out_specs = (P(None, "tile", "grp", "chan"), P("grp", None, None))
    return jax.shard_map(
        functools.partial(local_step, dict(mesh.shape)), mesh=mesh, in_specs=in_specs, out_specs=out_specs, check_vma=False
    )
```
